32 devices in a mesh: groups: 2 (over x), seg: 8 (over z, y), space: 2 (over core).
Axes of the slice: x: 2, y: 2, z: 4, core: 2. Of those that a mesh axis runs over, the one named last changes fastest.
Arguments:
- trajectory: float32 [16, 32, 2, 16, 256], P(('groups', 'seg'), None, None, 'space'), parts along dimension 0, may hold values from -3 to 3
Outputs:
- corrected: float32 [16, 32, 2, 16, 256], P(('groups', 'seg'), None, None, 'space'), parts along dimension 0
The draws below stay inside these ranges and needn't reach their ends.
There are 2 independent parts, one for each index of `groups`. The reference program is written for one: setup_inputs(seed, part) draws one part's arguments, and reference() takes and returns one part's arrays. A program takes and returns all parts, laid end to end along the dimension named above; each array names one. Nothing has to cross between parts.
All inputs are finite; a program needn't handle non-finite values.
Results may differ from the reference program's by a relative error of at most 0.0003.
Values sent between devices are 32-bit elements; how exact they have to be, the bound alone decides.
A program may use at most 64 MiB of HBM per device.

```python
import jax
import jax.numpy as jnp
import numpy as np
from jax import lax

NY = 256
NODES = 32
SWEEPS = 3
CSTEPS = 4
COARSEN = 4
SEGS = 8
NX = 16


def steps_of(key, shape, cuts, least, high):
    factor_of, own = 1.0, jax.random.fold_in(key, 6)
    for dim, shards_of in cuts:
        steps = jnp.exp(jax.random.uniform(jax.random.fold_in(own, dim), (shards_of,), jnp.float32, least / len(cuts), high / len(cuts)))
        factor_of = factor_of * jnp.repeat(steps, shape[dim] // shards_of).reshape([-1 if axis == dim else 1 for axis in range(len(shape))])
    return factor_of


def bell_draw(own_key, dims, deviation, reach, cuts=(), held_as=jnp.bfloat16):
    drawn = deviation * jax.random.normal(own_key, dims, jnp.float32)
    if cuts:
        drawn = drawn * steps_of(own_key, dims, cuts, -0.22, 0.18)
    return jnp.clip(drawn, -reach, reach).astype(held_as)


def setup_inputs(seed: int = 0, part: int = 0) -> dict:
    streams_of = jax.random.split(jax.random.key(seed), 2)
    own_keys = jax.random.split(jax.random.fold_in(streams_of[1], part), 2)
    return {
        "trajectory": bell_draw(own_keys[0], (SEGS, NODES, 2, NX, NY), 0.5, 3.0, ((0, 8), (3, 2)), jnp.float32),
    }


SEGMENT_TIME = 0.5
VISCOSITY = 0.05


def integration_table(count, length):
    last = count - 1
    orders = np.arange(count)
    angles = np.pi * (last - orders) / last
    points = np.cos(angles)
    cheb = np.cos(np.outer(angles, orders))
    weights = np.where((orders == 0) | (orders == last), 0.5, 1.0)
    inverse = (2.0 / last) * weights[:, None] * cheb.T * weights[None, :]
    upper = orders + 1.0
    lower = np.maximum(orders - 1.0, 1.0)
    general = np.cos(np.outer(angles, upper)) / (2.0 * upper) - np.cos(np.outer(angles, orders - 1.0)) / (2.0 * lower)
    general = general - ((-1.0) ** (orders + 1) / (2.0 * upper) - (-1.0) ** np.abs(orders - 1) / (2.0 * lower))
    integral = np.where(orders[None, :] == 0, points[:, None] + 1.0, np.where(orders[None, :] == 1, (points[:, None] ** 2 - 1.0) / 2.0, general))
    return (integral @ inverse * (length / 2.0)).astype(np.float32)


def wrap_rows(field, width):
    return jnp.concatenate([field[..., -width:, :], field, field[..., :width, :]], axis=-2)


def burgers_rhs(padded, spacing):
    center = padded[..., 1:-1, :]
    north = padded[..., 2:, :]
    south = padded[..., :-2, :]
    east = jnp.roll(center, -1, axis=-1)
    west = jnp.roll(center, 1, axis=-1)
    grad_x = (north - south) / (2.0 * spacing)
    grad_y = (east - west) / (2.0 * spacing)
    lapl = (north + south + east + west - 4.0 * center) / (spacing * spacing)
    vel_u = center[..., 0:1, :, :]
    vel_v = center[..., 1:2, :, :]
    return VISCOSITY * lapl - (vel_u * grad_x + vel_v * grad_y)


def picard_sweep(padded, int_table):
    slope = burgers_rhs(padded, 1.0)
    begin = padded[0:1, :, 1:-1, :]
    flat_slope = slope.reshape(slope.shape[0], -1)
    integral = jnp.dot(int_table, flat_slope, precision=lax.Precision.HIGHEST)
    return begin + integral.reshape(slope.shape)


def restrict(field):
    shaped = field.reshape(field.shape[:-2] + (field.shape[-2] // COARSEN, COARSEN, field.shape[-1] // COARSEN, COARSEN))
    return jnp.mean(shaped, axis=(-3, -1))


def prolong(field):
    return jnp.repeat(jnp.repeat(field, COARSEN, axis=-2), COARSEN, axis=-1)


def coarse_prop(coarse_now):
    step_len = SEGMENT_TIME / CSTEPS
    for number in range(CSTEPS):
        coarse_now = coarse_now + step_len * burgers_rhs(wrap_rows(coarse_now, 1), float(COARSEN))
    return coarse_now


def reference(trajectory):
    int_table = jnp.asarray(integration_table(NODES, SEGMENT_TIME))

    def fine(segment):
        current = segment
        for number in range(SWEEPS):
            current = picard_sweep(wrap_rows(current, 1), int_table)
        return current

    swept = lax.map(fine, trajectory)
    ends = swept[:, -1]
    r_start = restrict(trajectory[:, 0])
    jumps = restrict(ends) - lax.map(coarse_prop, r_start)

    def chain(carry, jump_now):
        nxt = coarse_prop(carry) + jump_now
        return nxt, nxt

    last, later = lax.scan(chain, r_start[0], jumps[:-1])
    prev_end = ends[:-1]
    fixed = (prev_end + prolong(later - restrict(prev_end))) - trajectory[1:, 0]
    shift_all = jnp.concatenate([jnp.zeros_like(fixed[:1]), fixed], axis=0)
    return swept + shift_all[:, None]
```

```python
import functools

import jax
import jax.numpy as jnp
import ml_dtypes
import numpy as np
from jax import lax
from jax.experimental import pallas as pl
from jax.experimental.pallas import tpu as pltpu
from jax.sharding import PartitionSpec as P

SWEEPS = 3
CSTEPS = 4
COARSEN = 4
SEGMENT_TIME = 0.5
VISCOSITY = 0.05
MESH = pl.DeviceIdType.MESH
CHUNKS = 4


def integration_table(count, length):
    last = count - 1
    orders = np.arange(count)
    angles = np.pi * (last - orders) / last
    points = np.cos(angles)
    cheb = np.cos(np.outer(angles, orders))
    weights = np.where((orders == 0) | (orders == last), 0.5, 1.0)
    inverse = 2.0 / last * weights[:, None] * cheb.T * weights[None, :]
    upper = orders + 1.0
    lower = np.maximum(orders - 1.0, 1.0)
    general = np.cos(np.outer(angles, upper)) / (2.0 * upper) - np.cos(
        np.outer(angles, orders - 1.0)
    ) / (2.0 * lower)
    general = general - (
        (-1.0) ** (orders + 1) / (2.0 * upper) - (-1.0) ** np.abs(orders - 1) / (2.0 * lower)
    )
    integral = np.where(
        orders[None, :] == 0,
        points[:, None] + 1.0,
        np.where(orders[None, :] == 1, (points[:, None] ** 2 - 1.0) / 2.0, general),
    )
    return (integral @ inverse * (length / 2.0)).astype(np.float32)


def split2(x):
    hi = x.astype(jnp.bfloat16)
    lo = (x - hi.astype(jnp.float32)).astype(jnp.bfloat16)
    return hi, lo


def tables(nodes, rows, cols):
    table = integration_table(nodes, SEGMENT_TIME)
    hi = table.astype(ml_dtypes.bfloat16)
    lo = (table - hi.astype(np.float32)).astype(ml_dtypes.bfloat16)
    eye = np.eye(rows, dtype=np.float32)
    big_hi = np.kron(hi.astype(np.float32), eye)
    big_lo = np.kron(lo.astype(np.float32), eye)
    big = np.concatenate([big_hi, big_hi, big_lo], axis=1).astype(ml_dtypes.bfloat16)
    coarse = cols // COARSEN
    fine_of = np.arange(cols)[:, None] // COARSEN
    copies = np.arange(2 * coarse)[None, :] % coarse
    down = (fine_of == copies).astype(np.float32) / (COARSEN * COARSEN)
    down = np.concatenate([down, down], axis=0).astype(ml_dtypes.bfloat16)
    up = (fine_of == copies).astype(np.float32).T.astype(ml_dtypes.bfloat16)
    return big, down, up


def coarse_prop(u, v):
    step_len = SEGMENT_TIME / CSTEPS
    spacing = float(COARSEN)
    a = step_len * VISCOSITY / (spacing * spacing)
    b = step_len / (2.0 * spacing)
    lanes = u.shape[1]
    for _ in range(CSTEPS):
        bu, bv = b * u, b * v
        cn, cs, ce, cw = a - bu, a + bu, a - bv, a + bv
        both = []
        for q in (u, v):
            north, south = pltpu.roll(q, 7, 0), pltpu.roll(q, 1, 0)
            east, west = pltpu.roll(q, lanes - 1, 1), pltpu.roll(q, 1, 1)
            both.append(
                ((1.0 - 4.0 * a) * q + (north * cn + south * cs)) + (east * ce + west * cw)
            )
        u, v = both
    return u, v


def row_sums(y):
    y = y + pltpu.roll(y, 1, 0)
    return y + pltpu.roll(y, 2, 0)


def kernel(
    nseg, x_hbm, t_hbm, r_hbm, p_hbm, swept_hbm, shift_ref,
    X, Sb, T, Rm, Pm, coarse0, jumps, prev, jsend, csend, ends,
    lsem, csem, xs_sem, xr_sem, js_sem, jr_sem, cs_sem, cr_sem, ps_sem, pr_sem, osem,
):
    seg = lax.axis_index("seg")
    space = lax.axis_index("space")
    other = 1 - space
    nodes, cols = X.shape[1], X.shape[4]
    rows = X.shape[3]
    per = nodes // CHUNKS
    depth = nodes * rows
    half = Rm.shape[1] // 2

    loads = []
    for c in range(CHUNKS):
        part = pl.ds(c * per, per)
        loads.append(pltpu.make_async_copy(x_hbm.at[0, part], X.at[0, part], lsem.at[c]))
        loads[-1].start()
    consts = [
        pltpu.make_async_copy(r_hbm, Rm, csem.at[0]),
        pltpu.make_async_copy(t_hbm, T, csem.at[1]),
        pltpu.make_async_copy(p_hbm, Pm, csem.at[2]),
    ]
    for copy in consts:
        copy.start()

    barrier = pltpu.get_barrier_semaphore()
    pl.semaphore_signal(
        barrier, inc=1, device_id={"space": other}, device_id_type=MESH
    )

    def greet(t, _):
        for s in range(2):
            pl.semaphore_signal(
                barrier, inc=1, device_id={"seg": t, "space": s}, device_id_type=MESH
            )
        return 0

    lax.fori_loop(0, seg, greet, 0)
    pl.semaphore_wait(barrier, 2 * (nseg - 1 - seg) + 1)

    swaps = []
    for c in range(CHUNKS):
        part = pl.ds(c * per, per)
        swaps.append(
            pltpu.make_async_remote_copy(
                src_ref=x_hbm.at[0, part], dst_ref=X.at[1, part],
                send_sem=xs_sem.at[c], recv_sem=xr_sem.at[c],
                device_id={"space": other}, device_id_type=MESH,
            )
        )
        swaps[-1].start()

    row_id = lax.broadcasted_iota(jnp.int32, (rows, cols), 0)
    top, bottom = row_id == rows - 1, row_id == 0
    lane_id = lax.broadcasted_iota(jnp.int32, (8, 2 * half), 1)
    left = lane_id < half

    def slope_pair(q_own, q_oth):
        up_own, up_oth = pltpu.roll(q_own, rows - 1, 0), pltpu.roll(q_oth, rows - 1, 0)
        dn_own, dn_oth = pltpu.roll(q_own, 1, 0), pltpu.roll(q_oth, 1, 0)
        return (
            (jnp.where(top, up_oth, up_own), jnp.where(bottom, dn_oth, dn_own)),
            (jnp.where(top, up_own, up_oth), jnp.where(bottom, dn_own, dn_oth)),
        )

    def node_slopes(m, strips):
        fields = [[X[s, m, c] for c in range(2)] for s in range(2)]
        vert = [slope_pair(fields[0][c], fields[1][c]) for c in range(2)]
        out = []
        for s in range(strips):
            hu, hv = 0.5 * fields[s][0], 0.5 * fields[s][1]
            cn, cs, ce, cw = VISCOSITY - hu, VISCOSITY + hu, VISCOSITY - hv, VISCOSITY + hv
            for c in range(2):
                q = fields[s][c]
                north, south = vert[c][s]
                east, west = pltpu.roll(q, cols - 1, 1), pltpu.roll(q, 1, 1)
                out.append(
                    (north * cn + south * cs)
                    + (east * ce + west * cw)
                    - (4.0 * VISCOSITY) * q
                )
        return out

    def slopes(first, count, strips):
        def body(j, _):
            m = 2 * j
            one, two = node_slopes(m, strips), node_slopes(m + 1, strips)
            for b in range(2 * strips):
                both = jnp.concatenate([one[b], two[b]], axis=0)
                hi, lo = split2(both)
                at = pl.multiple_of(j * (2 * rows), 2 * rows)
                lanes = pl.ds(b * cols, cols)
                Sb[pl.ds(at, 2 * rows), lanes] = hi
                Sb[pl.ds(depth + at, 2 * rows), lanes] = lo
                Sb[pl.ds(2 * depth + at, 2 * rows), lanes] = hi
            return 0

        lax.fori_loop(first // 2, (first + count) // 2, body, 0)

    def integrate(strips):
        for b in range(2 * strips):
            s, c = divmod(b, 2)
            total = jnp.dot(
                T[...], Sb[:, b * cols : (b + 1) * cols], preferred_element_type=jnp.float32
            )
            X[s, :, c] = X[s, 0, c][None] + total.reshape(nodes, rows, cols)

    def restrict_lanes(stack):
        hi, lo = split2(stack)
        return jnp.dot(
            jnp.concatenate([hi, lo], axis=1), Rm[...], preferred_element_type=jnp.float32
        )

    for c in range(CHUNKS):
        loads[c].wait()
        swaps[c].wait_recv()
        slopes(c * per, per, 2)

    consts[0].wait()
    starts = restrict_lanes(
        jnp.concatenate([X[0, 0, 0], X[0, 0, 1], X[1, 0, 0], X[1, 0, 1]], axis=0)
    )
    sums = [row_sums(starts[8 * b : 8 * b + 8]) for b in range(4)]

    def ends_of(y):
        return [y[3:4], y[7:8]]

    su = jnp.concatenate((ends_of(sums[0]) + ends_of(sums[2])) * 2, axis=0)
    sv = jnp.concatenate((ends_of(sums[1]) + ends_of(sums[3])) * 2, axis=0)
    packed = jnp.where(left, su, sv)
    csend[...] = packed[0:4]

    def coarse_copy(t):
        return pltpu.make_async_remote_copy(
            src_ref=csend, dst_ref=coarse0, send_sem=cs_sem.at[t], recv_sem=cr_sem,
            device_id={"seg": t}, device_id_type=MESH,
        )

    @pl.when(seg == 0)
    def _():
        for t in range(nseg - 1, 0, -1):
            coarse_copy(t).start()

    gu, gv = coarse_prop(su, sv)
    gpack = jnp.where(left, gu, gv)

    consts[1].wait()
    integrate(2)
    slopes(0, nodes, 2)
    integrate(2)
    slopes(0, nodes, 1)

    tail = jnp.dot(
        T[depth - 2 * rows :, :], Sb[:, : 2 * cols], preferred_element_type=jnp.float32
    )[rows:]
    eu = X[0, 0, 0] + tail[:, :cols]
    ev = X[0, 0, 1] + tail[:, cols:]
    ends[0] = eu
    ends[1] = ev
    finish = restrict_lanes(jnp.concatenate([eu, ev], axis=0))
    fpack = row_sums(jnp.where(left, finish[:8], finish[8:]))
    jsend[0:1] = fpack[3:4] - gpack[0:1]
    jsend[1:2] = fpack[7:8] - gpack[1:2]

    def jump_copy(t, s, way):
        return pltpu.make_async_remote_copy(
            src_ref=jsend, dst_ref=jumps.at[seg, way],
            send_sem=js_sem.at[t, way], recv_sem=jr_sem.at[seg, way],
            device_id={"seg": t, "space": s}, device_id_type=MESH,
        )

    def send_jump(i, _):
        t = nseg - 1 - i
        jump_copy(t, space, 0).start()
        jump_copy(t, other, 1).start()
        return 0

    lax.fori_loop(0, nseg - 1 - seg, send_jump, 0)

    end_copy = pltpu.make_async_remote_copy(
        src_ref=ends, dst_ref=prev, send_sem=ps_sem, recv_sem=pr_sem,
        device_id={"seg": lax.rem(seg + 1, nseg)}, device_id_type=MESH,
    )

    @pl.when(seg < nseg - 1)
    def _():
        end_copy.start()

    integrate(1)
    store = pltpu.make_async_copy(X.at[0], swept_hbm, osem)
    store.start()
    consts[2].wait()

    def expand(x):
        y = pltpu.roll(x, half, 1)
        return jnp.where(left, x, y), jnp.where(left, y, x)

    @pl.when(seg == 0)
    def _():
        shift_ref[...] = jnp.zeros_like(shift_ref)

    @pl.when(seg > 0)
    def _():
        coarse_copy(0).wait_recv()
        c = coarse0[...]
        u, v = expand(jnp.concatenate([c, c], axis=0))

        def advance(i, carry):
            u, v = coarse_prop(*carry)
            for way in range(2):
                pltpu.make_async_copy(jsend, jumps.at[i, way], jr_sem.at[i, way]).wait()
            own, oth = jumps[i, 0], jumps[i, 1]
            du, dv = expand(jnp.concatenate([own, oth, own, oth], axis=0))
            return u + du, v + dv

        u, v = lax.fori_loop(0, seg, advance, (u, v))
        end_copy.wait_recv()
        pu, pv = prev[0], prev[1]
        back = restrict_lanes(jnp.concatenate([pu, pv], axis=0))
        lower = lax.broadcasted_iota(jnp.int32, (8, 2 * half), 0) < 4
        spread = []
        for q, r in ((u, row_sums(back[:8])), (v, row_sums(back[8:]))):
            d0 = jnp.broadcast_to(q[0:1] - r[3:4], (8, 2 * half))
            d1 = jnp.broadcast_to(q[1:2] - r[7:8], (8, 2 * half))
            hi, lo = split2(jnp.where(lower, d0, d1))
            spread.append(
                jnp.where(left, hi.astype(jnp.float32), lo.astype(jnp.float32))
            )
        wide = jnp.dot(
            jnp.concatenate(spread, axis=0).astype(jnp.bfloat16), Pm[...],
            preferred_element_type=jnp.float32,
        )
        shift_ref[0] = (pu + wide[:8]) - X[0, 0, 0]
        shift_ref[1] = (pv + wide[8:]) - X[0, 0, 1]

    for copy in swaps:
        copy.wait_send()

    @pl.when(seg == 0)
    def _():
        for t in range(nseg - 1, 0, -1):
            coarse_copy(t).wait_send()

    def sent(i, _):
        t = nseg - 1 - i
        jump_copy(t, space, 0).wait_send()
        jump_copy(t, other, 1).wait_send()
        return 0

    lax.fori_loop(0, nseg - 1 - seg, sent, 0)

    @pl.when(seg < nseg - 1)
    def _():
        end_copy.wait_send()

    store.wait()


def per_device(nseg, trajectory):
    _, nodes, comps, rows, cols = trajectory.shape
    big, down, up = tables(nodes, rows, cols)
    depth = nodes * rows
    half = cols // COARSEN
    crows = rows // COARSEN
    bf16, f32 = jnp.bfloat16, jnp.float32
    DMA = pltpu.SemaphoreType.DMA
    anywhere = pl.BlockSpec(memory_space=pl.ANY)
    swept, shift = pl.pallas_call(
        functools.partial(kernel, nseg),
        out_shape=(
            jax.ShapeDtypeStruct((nodes, comps, rows, cols), f32),
            jax.ShapeDtypeStruct((comps, rows, cols), f32),
        ),
        in_specs=[anywhere] * 4,
        out_specs=(anywhere, pl.BlockSpec(memory_space=pltpu.VMEM)),
        scratch_shapes=[
            pltpu.VMEM((2, nodes, comps, rows, cols), f32),
            pltpu.VMEM((3 * depth, 2 * comps * cols), bf16),
            pltpu.VMEM(big.shape, bf16),
            pltpu.VMEM(down.shape, bf16),
            pltpu.VMEM(up.shape, bf16),
            pltpu.VMEM((2 * crows, 2 * half), f32),
            pltpu.VMEM((nseg, 2, crows, 2 * half), f32),
            pltpu.VMEM((comps, rows, cols), f32),
            pltpu.VMEM((crows, 2 * half), f32),
            pltpu.VMEM((2 * crows, 2 * half), f32),
            pltpu.VMEM((comps, rows, cols), f32),
            DMA((CHUNKS,)), DMA((3,)), DMA((CHUNKS,)), DMA((CHUNKS,)),
            DMA((nseg, 2)), DMA((nseg, 2)), DMA((nseg,)), DMA, DMA, DMA, DMA,
        ],
        compiler_params=pltpu.CompilerParams(
            collective_id=0, has_side_effects=True, vmem_limit_bytes=24 * 2**20
        ),
    )(trajectory, jnp.asarray(big), jnp.asarray(down), jnp.asarray(up))
    return (swept + shift[None])[None]


def solution(mesh):
    spec = P(("groups", "seg"), None, None, "space", None)
    return jax.shard_map(
        functools.partial(per_device, mesh.shape["seg"]),
        mesh=mesh,
        in_specs=(spec,),
        out_specs=spec,
        check_vma=False,
    )
```

```python
import functools

import jax
import jax.numpy as jnp
import ml_dtypes
import numpy as np
from jax import lax
from jax.experimental import pallas as pl
from jax.experimental.pallas import tpu as pltpu
from jax.sharding import PartitionSpec as P

SWEEPS = 3
CSTEPS = 4
COARSEN = 4
SEGMENT_TIME = 0.5
VISCOSITY = 0.05
MESH = pl.DeviceIdType.MESH
CHUNKS = 4


def integration_table(count, length):
    last = count - 1
    orders = np.arange(count)
    angles = np.pi * (last - orders) / last
    points = np.cos(angles)
    cheb = np.cos(np.outer(angles, orders))
    weights = np.where((orders == 0) | (orders == last), 0.5, 1.0)
    inverse = 2.0 / last * weights[:, None] * cheb.T * weights[None, :]
    upper = orders + 1.0
    lower = np.maximum(orders - 1.0, 1.0)
    general = np.cos(np.outer(angles, upper)) / (2.0 * upper) - np.cos(
        np.outer(angles, orders - 1.0)
    ) / (2.0 * lower)
    general = general - (
        (-1.0) ** (orders + 1) / (2.0 * upper) - (-1.0) ** np.abs(orders - 1) / (2.0 * lower)
    )
    integral = np.where(
        orders[None, :] == 0,
        points[:, None] + 1.0,
        np.where(orders[None, :] == 1, (points[:, None] ** 2 - 1.0) / 2.0, general),
    )
    return (integral @ inverse * (length / 2.0)).astype(np.float32)


def split2(x):
    hi = x.astype(jnp.bfloat16)
    lo = (x - hi.astype(jnp.float32)).astype(jnp.bfloat16)
    return hi, lo


def tables(nodes, rows, cols):
    table = integration_table(nodes, SEGMENT_TIME)
    hi = table.astype(ml_dtypes.bfloat16)
    lo = (table - hi.astype(np.float32)).astype(ml_dtypes.bfloat16)
    eye = np.eye(rows, dtype=np.float32)
    big_hi = np.kron(hi.astype(np.float32), eye)
    big_lo = np.kron(lo.astype(np.float32), eye)
    big = np.concatenate([big_hi, big_hi, big_lo], axis=1).astype(ml_dtypes.bfloat16)
    coarse = cols // COARSEN
    fine_of = np.arange(cols)[:, None] // COARSEN
    copies = np.arange(2 * coarse)[None, :] % coarse
    down = (fine_of == copies).astype(np.float32) / (COARSEN * COARSEN)
    down = np.concatenate([down, down], axis=0).astype(ml_dtypes.bfloat16)
    up = (fine_of == copies).astype(np.float32).T.astype(ml_dtypes.bfloat16)
    return big, down, up


def coarse_prop(u, v):
    step_len = SEGMENT_TIME / CSTEPS
    spacing = float(COARSEN)
    a = step_len * VISCOSITY / (spacing * spacing)
    b = step_len / (2.0 * spacing)
    lanes = u.shape[1]
    for _ in range(CSTEPS):
        bu, bv = b * u, b * v
        cn, cs, ce, cw = a - bu, a + bu, a - bv, a + bv
        both = []
        for q in (u, v):
            north, south = pltpu.roll(q, 7, 0), pltpu.roll(q, 1, 0)
            east, west = pltpu.roll(q, lanes - 1, 1), pltpu.roll(q, 1, 1)
            both.append(
                ((1.0 - 4.0 * a) * q + (north * cn + south * cs)) + (east * ce + west * cw)
            )
        u, v = both
    return u, v


def row_sums(y):
    y = y + pltpu.roll(y, 1, 0)
    return y + pltpu.roll(y, 2, 0)


def kernel(
    nseg, x_hbm, t_hbm, r_hbm, p_hbm, swept_hbm, shift_ref,
    X, Sb, T, Rm, Pm, coarse0, jumps, prev, jsend, csend, ends,
    lsem, csem, xs_sem, xr_sem, js_sem, jr_sem, cs_sem, cr_sem, ps_sem, pr_sem, osem,
    hello, ready,
):
    seg = lax.axis_index("seg")
    space = lax.axis_index("space")
    other = 1 - space
    nodes, cols = X.shape[1], X.shape[4]
    rows = X.shape[3]
    per = nodes // CHUNKS
    depth = nodes * rows
    half = Rm.shape[1] // 2

    loads = []
    for c in range(CHUNKS):
        part = pl.ds(c * per, per)
        loads.append(pltpu.make_async_copy(x_hbm.at[0, part], X.at[0, part], lsem.at[c]))
        loads[-1].start()
    consts = [
        pltpu.make_async_copy(r_hbm, Rm, csem.at[0]),
        pltpu.make_async_copy(t_hbm, T, csem.at[1]),
        pltpu.make_async_copy(p_hbm, Pm, csem.at[2]),
    ]
    for copy in consts:
        copy.start()

    barrier = pltpu.get_barrier_semaphore()

    @pl.when(space == 0)
    def _():
        pl.semaphore_signal(
            barrier, inc=1, device_id={"space": 1}, device_id_type=MESH
        )

    def greet(t, _):
        pl.semaphore_signal(
            barrier, inc=1, device_id={"seg": t, "space": 0}, device_id_type=MESH
        )
        return 0

    lax.fori_loop(0, seg, greet, 0)

    @pl.when(space == 1)
    def _():
        pl.semaphore_wait(barrier, 1)
        pl.semaphore_signal(
            hello, inc=1, device_id={"space": 0}, device_id_type=MESH
        )

    @pl.when(space == 0)
    def _():
        pl.semaphore_wait(hello, 1)

    swaps = []
    for c in range(CHUNKS):
        part = pl.ds(c * per, per)
        swaps.append(
            pltpu.make_async_remote_copy(
                src_ref=x_hbm.at[0, part], dst_ref=X.at[1, part],
                send_sem=xs_sem.at[c], recv_sem=xr_sem.at[c],
                device_id={"space": other}, device_id_type=MESH,
            )
        )
        swaps[-1].start()

    row_id = lax.broadcasted_iota(jnp.int32, (rows, cols), 0)
    top, bottom = row_id == rows - 1, row_id == 0
    lane_id = lax.broadcasted_iota(jnp.int32, (8, 2 * half), 1)
    left = lane_id < half

    def slope_pair(q_own, q_oth):
        up_own, up_oth = pltpu.roll(q_own, rows - 1, 0), pltpu.roll(q_oth, rows - 1, 0)
        dn_own, dn_oth = pltpu.roll(q_own, 1, 0), pltpu.roll(q_oth, 1, 0)
        return (
            (jnp.where(top, up_oth, up_own), jnp.where(bottom, dn_oth, dn_own)),
            (jnp.where(top, up_own, up_oth), jnp.where(bottom, dn_own, dn_oth)),
        )

    def node_slopes(m, strips):
        fields = [[X[s, m, c] for c in range(2)] for s in range(2)]
        vert = [slope_pair(fields[0][c], fields[1][c]) for c in range(2)]
        out = []
        for s in range(strips):
            hu, hv = 0.5 * fields[s][0], 0.5 * fields[s][1]
            cn, cs, ce, cw = VISCOSITY - hu, VISCOSITY + hu, VISCOSITY - hv, VISCOSITY + hv
            for c in range(2):
                q = fields[s][c]
                north, south = vert[c][s]
                east, west = pltpu.roll(q, cols - 1, 1), pltpu.roll(q, 1, 1)
                out.append(
                    (north * cn + south * cs)
                    + (east * ce + west * cw)
                    - (4.0 * VISCOSITY) * q
                )
        return out

    def slopes(first, count, strips):
        def body(j, _):
            m = 2 * j
            one, two = node_slopes(m, strips), node_slopes(m + 1, strips)
            for b in range(2 * strips):
                both = jnp.concatenate([one[b], two[b]], axis=0)
                hi, lo = split2(both)
                at = pl.multiple_of(j * (2 * rows), 2 * rows)
                lanes = pl.ds(b * cols, cols)
                Sb[pl.ds(at, 2 * rows), lanes] = hi
                Sb[pl.ds(depth + at, 2 * rows), lanes] = lo
                Sb[pl.ds(2 * depth + at, 2 * rows), lanes] = hi
            return 0

        lax.fori_loop(first // 2, (first + count) // 2, body, 0, unroll=4)

    def integrate(strips):
        for b in range(2 * strips):
            s, c = divmod(b, 2)
            total = jnp.dot(
                T[...], Sb[:, b * cols : (b + 1) * cols], preferred_element_type=jnp.float32
            )
            X[s, :, c] = X[s, 0, c][None] + total.reshape(nodes, rows, cols)

    def restrict_lanes(stack):
        hi, lo = split2(stack)
        return jnp.dot(
            jnp.concatenate([hi, lo], axis=1), Rm[...], preferred_element_type=jnp.float32
        )

    for c in range(CHUNKS):
        loads[c].wait()
        swaps[c].wait_recv()
        slopes(c * per, per, 2)

    consts[0].wait()
    starts = restrict_lanes(
        jnp.concatenate([X[0, 0, 0], X[0, 0, 1], X[1, 0, 0], X[1, 0, 1]], axis=0)
    )
    sums = [row_sums(starts[8 * b : 8 * b + 8]) for b in range(4)]

    def ends_of(y):
        return [y[3:4], y[7:8]]

    su = jnp.concatenate((ends_of(sums[0]) + ends_of(sums[2])) * 2, axis=0)
    sv = jnp.concatenate((ends_of(sums[1]) + ends_of(sums[3])) * 2, axis=0)
    packed = jnp.where(left, su, sv)
    csend[...] = packed[0:4]

    def coarse_copy(t):
        return pltpu.make_async_remote_copy(
            src_ref=csend, dst_ref=coarse0, send_sem=cs_sem.at[t], recv_sem=cr_sem,
            device_id={"seg": t}, device_id_type=MESH,
        )

    gu, gv = coarse_prop(su, sv)
    gpack = jnp.where(left, gu, gv)

    consts[1].wait()
    integrate(2)
    slopes(0, nodes, 2)
    integrate(2)
    slopes(0, nodes, 1)

    @pl.when(seg < nseg - 1)
    def _():
        @pl.when(space == 0)
        def _():
            pl.semaphore_wait(barrier, 2 * (nseg - 1 - seg))
            pl.semaphore_signal(
                ready, inc=1, device_id={"space": 1}, device_id_type=MESH
            )

        @pl.when(space == 1)
        def _():
            pl.semaphore_wait(ready, 1)

    @pl.when(seg == 0)
    def _():
        for t in range(nseg - 1, 0, -1):
            coarse_copy(t).start()

    tail = jnp.dot(
        T[depth - 2 * rows :, :], Sb[:, : 2 * cols], preferred_element_type=jnp.float32
    )[rows:]
    eu = X[0, 0, 0] + tail[:, :cols]
    ev = X[0, 0, 1] + tail[:, cols:]
    ends[0] = eu
    ends[1] = ev
    finish = restrict_lanes(jnp.concatenate([eu, ev], axis=0))
    fpack = row_sums(jnp.where(left, finish[:8], finish[8:]))
    jsend[0:1] = fpack[3:4] - gpack[0:1]
    jsend[1:2] = fpack[7:8] - gpack[1:2]

    def jump_copy(t, s, way):
        return pltpu.make_async_remote_copy(
            src_ref=jsend, dst_ref=jumps.at[seg, way],
            send_sem=js_sem.at[t, way], recv_sem=jr_sem.at[seg, way],
            device_id={"seg": t, "space": s}, device_id_type=MESH,
        )

    def send_jump(i, _):
        t = nseg - 1 - i
        jump_copy(t, space, 0).start()
        jump_copy(t, other, 1).start()
        return 0

    lax.fori_loop(0, nseg - 1 - seg, send_jump, 0)

    end_copy = pltpu.make_async_remote_copy(
        src_ref=ends, dst_ref=prev, send_sem=ps_sem, recv_sem=pr_sem,
        device_id={"seg": lax.rem(seg + 1, nseg)}, device_id_type=MESH,
    )

    @pl.when(seg < nseg - 1)
    def _():
        end_copy.start()

    integrate(1)
    store = pltpu.make_async_copy(X.at[0], swept_hbm, osem)
    store.start()
    consts[2].wait()

    def expand(x):
        y = pltpu.roll(x, half, 1)
        return jnp.where(left, x, y), jnp.where(left, y, x)

    @pl.when(seg == 0)
    def _():
        shift_ref[...] = jnp.zeros_like(shift_ref)

    @pl.when(seg > 0)
    def _():
        coarse_copy(0).wait_recv()
        c = coarse0[...]
        u, v = expand(jnp.concatenate([c, c], axis=0))

        def advance(i, carry):
            u, v = coarse_prop(*carry)
            for way in range(2):
                pltpu.make_async_copy(jsend, jumps.at[i, way], jr_sem.at[i, way]).wait()
            own, oth = jumps[i, 0], jumps[i, 1]
            du, dv = expand(jnp.concatenate([own, oth, own, oth], axis=0))
            return u + du, v + dv

        u, v = lax.fori_loop(0, seg, advance, (u, v))
        end_copy.wait_recv()
        pu, pv = prev[0], prev[1]
        back = restrict_lanes(jnp.concatenate([pu, pv], axis=0))
        lower = lax.broadcasted_iota(jnp.int32, (8, 2 * half), 0) < 4
        spread = []
        for q, r in ((u, row_sums(back[:8])), (v, row_sums(back[8:]))):
            d0 = jnp.broadcast_to(q[0:1] - r[3:4], (8, 2 * half))
            d1 = jnp.broadcast_to(q[1:2] - r[7:8], (8, 2 * half))
            hi, lo = split2(jnp.where(lower, d0, d1))
            spread.append(
                jnp.where(left, hi.astype(jnp.float32), lo.astype(jnp.float32))
            )
        wide = jnp.dot(
            jnp.concatenate(spread, axis=0).astype(jnp.bfloat16), Pm[...],
            preferred_element_type=jnp.float32,
        )
        shift_ref[0] = (pu + wide[:8]) - X[0, 0, 0]
        shift_ref[1] = (pv + wide[8:]) - X[0, 0, 1]

    for copy in swaps:
        copy.wait_send()

    @pl.when(seg == 0)
    def _():
        for t in range(nseg - 1, 0, -1):
            coarse_copy(t).wait_send()

    def sent(i, _):
        t = nseg - 1 - i
        jump_copy(t, space, 0).wait_send()
        jump_copy(t, other, 1).wait_send()
        return 0

    lax.fori_loop(0, nseg - 1 - seg, sent, 0)

    @pl.when(seg < nseg - 1)
    def _():
        end_copy.wait_send()

    store.wait()


def per_device(nseg, trajectory):
    _, nodes, comps, rows, cols = trajectory.shape
    big, down, up = tables(nodes, rows, cols)
    depth = nodes * rows
    half = cols // COARSEN
    crows = rows // COARSEN
    bf16, f32 = jnp.bfloat16, jnp.float32
    DMA = pltpu.SemaphoreType.DMA
    anywhere = pl.BlockSpec(memory_space=pl.ANY)
    swept, shift = pl.pallas_call(
        functools.partial(kernel, nseg),
        out_shape=(
            jax.ShapeDtypeStruct((nodes, comps, rows, cols), f32),
            jax.ShapeDtypeStruct((comps, rows, cols), f32),
        ),
        in_specs=[anywhere] * 4,
        out_specs=(anywhere, pl.BlockSpec(memory_space=pltpu.VMEM)),
        scratch_shapes=[
            pltpu.VMEM((2, nodes, comps, rows, cols), f32),
            pltpu.VMEM((3 * depth, 2 * comps * cols), bf16),
            pltpu.VMEM(big.shape, bf16),
            pltpu.VMEM(down.shape, bf16),
            pltpu.VMEM(up.shape, bf16),
            pltpu.VMEM((2 * crows, 2 * half), f32),
            pltpu.VMEM((nseg, 2, crows, 2 * half), f32),
            pltpu.VMEM((comps, rows, cols), f32),
            pltpu.VMEM((crows, 2 * half), f32),
            pltpu.VMEM((2 * crows, 2 * half), f32),
            pltpu.VMEM((comps, rows, cols), f32),
            DMA((CHUNKS,)), DMA((3,)), DMA((CHUNKS,)), DMA((CHUNKS,)),
            DMA((nseg, 2)), DMA((nseg, 2)), DMA((nseg,)), DMA, DMA, DMA, DMA,
            pltpu.SemaphoreType.REGULAR, pltpu.SemaphoreType.REGULAR,
        ],
        compiler_params=pltpu.CompilerParams(
            collective_id=0, has_side_effects=True, vmem_limit_bytes=60 * 2**20
        ),
    )(trajectory, jnp.asarray(big), jnp.asarray(down), jnp.asarray(up))
    return (swept + shift[None])[None]


def solution(mesh):
    spec = P(("groups", "seg"), None, None, "space", None)
    return jax.shard_map(
        functools.partial(per_device, mesh.shape["seg"]),
        mesh=mesh,
        in_specs=(spec,),
        out_specs=spec,
        check_vma=False,
    )
```

```python
import functools

import jax
import jax.numpy as jnp
import ml_dtypes
import numpy as np
from jax import lax
from jax.experimental import pallas as pl
from jax.experimental.pallas import tpu as pltpu
from jax.sharding import PartitionSpec as P

SWEEPS = 3
CSTEPS = 4
COARSEN = 4
SEGMENT_TIME = 0.5
VISCOSITY = 0.05
MESH = pl.DeviceIdType.MESH
CHUNKS = 4


def integration_table(count, length):
    last = count - 1
    orders = np.arange(count)
    angles = np.pi * (last - orders) / last
    points = np.cos(angles)
    cheb = np.cos(np.outer(angles, orders))
    weights = np.where((orders == 0) | (orders == last), 0.5, 1.0)
    inverse = 2.0 / last * weights[:, None] * cheb.T * weights[None, :]
    upper = orders + 1.0
    lower = np.maximum(orders - 1.0, 1.0)
    general = np.cos(np.outer(angles, upper)) / (2.0 * upper) - np.cos(
        np.outer(angles, orders - 1.0)
    ) / (2.0 * lower)
    general = general - (
        (-1.0) ** (orders + 1) / (2.0 * upper) - (-1.0) ** np.abs(orders - 1) / (2.0 * lower)
    )
    integral = np.where(
        orders[None, :] == 0,
        points[:, None] + 1.0,
        np.where(orders[None, :] == 1, (points[:, None] ** 2 - 1.0) / 2.0, general),
    )
    return (integral @ inverse * (length / 2.0)).astype(np.float32)


def split2(x):
    hi = x.astype(jnp.bfloat16)
    lo = (x - hi.astype(jnp.float32)).astype(jnp.bfloat16)
    return hi, lo


def tables(nodes, rows, cols):
    table = integration_table(nodes, SEGMENT_TIME)
    hi = table.astype(ml_dtypes.bfloat16)
    lo = (table - hi.astype(np.float32)).astype(ml_dtypes.bfloat16)
    eye = np.eye(rows, dtype=np.float32)
    big_hi = np.kron(hi.astype(np.float32), eye)
    big_lo = np.kron(lo.astype(np.float32), eye)
    big = np.concatenate([big_hi, big_hi, big_lo], axis=1).astype(ml_dtypes.bfloat16)
    coarse = cols // COARSEN
    fine_of = np.arange(cols)[:, None] // COARSEN
    copies = np.arange(2 * coarse)[None, :] % coarse
    down = (fine_of == copies).astype(np.float32) / (COARSEN * COARSEN)
    down = np.concatenate([down, down], axis=0).astype(ml_dtypes.bfloat16)
    up = (fine_of == copies).astype(np.float32).T.astype(ml_dtypes.bfloat16)
    return big, down, up


def coarse_prop(u, v):
    step_len = SEGMENT_TIME / CSTEPS
    spacing = float(COARSEN)
    a = step_len * VISCOSITY / (spacing * spacing)
    b = step_len / (2.0 * spacing)
    lanes = u.shape[1]
    for _ in range(CSTEPS):
        bu, bv = b * u, b * v
        cn, cs, ce, cw = a - bu, a + bu, a - bv, a + bv
        both = []
        for q in (u, v):
            north, south = pltpu.roll(q, 7, 0), pltpu.roll(q, 1, 0)
            east, west = pltpu.roll(q, lanes - 1, 1), pltpu.roll(q, 1, 1)
            both.append(
                ((1.0 - 4.0 * a) * q + (north * cn + south * cs)) + (east * ce + west * cw)
            )
        u, v = both
    return u, v


def row_sums(y):
    y = y + pltpu.roll(y, 1, 0)
    return y + pltpu.roll(y, 2, 0)


def kernel(
    nseg, x_hbm, t_hbm, swept_hbm, shift_ref,
    X, Sb, T, Rm, Pm, coarse0, jumps, prev, jsend, csend, ends,
    lsem, csem, xs_sem, xr_sem, js_sem, jr_sem, cs_sem, cr_sem, ps_sem, pr_sem, osem,
    hello, ready,
):
    seg = lax.axis_index("seg")
    space = lax.axis_index("space")
    other = 1 - space
    nodes, cols = X.shape[1], X.shape[4]
    rows = X.shape[3]
    per = nodes // CHUNKS
    depth = nodes * rows
    half = Rm.shape[1] // 2

    loads = []
    for c in range(CHUNKS):
        part = pl.ds(c * per, per)
        loads.append(pltpu.make_async_copy(x_hbm.at[0, part], X.at[0, part], lsem.at[c]))
        loads[-1].start()
    wide, narrow = T.shape[1], Rm.shape[1]
    below = pl.ds(0, Pm.shape[0])
    consts = [
        pltpu.make_async_copy(
            t_hbm.at[:, pl.ds(wide, narrow)], Rm.at[pl.ds(0, cols)], csem.at[0]
        ),
        pltpu.make_async_copy(
            t_hbm.at[:, pl.ds(wide + narrow, narrow)], Rm.at[pl.ds(cols, cols)], csem.at[1]
        ),
        pltpu.make_async_copy(t_hbm.at[:, pl.ds(0, wide)], T, csem.at[2]),
        pltpu.make_async_copy(
            t_hbm.at[below, pl.ds(wide + 2 * narrow, cols)], Pm, csem.at[3]
        ),
    ]
    for copy in consts:
        copy.start()

    barrier = pltpu.get_barrier_semaphore()

    @pl.when(space == 0)
    def _():
        pl.semaphore_signal(
            barrier, inc=1, device_id={"space": 1}, device_id_type=MESH
        )

    def greet(t, _):
        pl.semaphore_signal(
            barrier, inc=1, device_id={"seg": t, "space": 0}, device_id_type=MESH
        )
        return 0

    lax.fori_loop(0, seg, greet, 0)

    @pl.when(space == 1)
    def _():
        pl.semaphore_wait(barrier, 1)
        pl.semaphore_signal(
            hello, inc=1, device_id={"space": 0}, device_id_type=MESH
        )

    @pl.when(space == 0)
    def _():
        pl.semaphore_wait(hello, 1)

    swaps = []
    for c in range(CHUNKS):
        part = pl.ds(c * per, per)
        swaps.append(
            pltpu.make_async_remote_copy(
                src_ref=x_hbm.at[0, part], dst_ref=X.at[1, part],
                send_sem=xs_sem.at[c], recv_sem=xr_sem.at[c],
                device_id={"space": other}, device_id_type=MESH,
            )
        )
        swaps[-1].start()

    row_id = lax.broadcasted_iota(jnp.int32, (rows, cols), 0)
    top, bottom = row_id == rows - 1, row_id == 0
    lane_id = lax.broadcasted_iota(jnp.int32, (8, 2 * half), 1)
    left = lane_id < half

    def slope_pair(q_own, q_oth):
        up_own, up_oth = pltpu.roll(q_own, rows - 1, 0), pltpu.roll(q_oth, rows - 1, 0)
        dn_own, dn_oth = pltpu.roll(q_own, 1, 0), pltpu.roll(q_oth, 1, 0)
        return (
            (jnp.where(top, up_oth, up_own), jnp.where(bottom, dn_oth, dn_own)),
            (jnp.where(top, up_own, up_oth), jnp.where(bottom, dn_own, dn_oth)),
        )

    def node_slopes(m, strips):
        fields = [[X[s, m, c] for c in range(2)] for s in range(2)]
        vert = [slope_pair(fields[0][c], fields[1][c]) for c in range(2)]
        out = []
        for s in range(strips):
            hu, hv = 0.5 * fields[s][0], 0.5 * fields[s][1]
            cn, cs, ce, cw = VISCOSITY - hu, VISCOSITY + hu, VISCOSITY - hv, VISCOSITY + hv
            for c in range(2):
                q = fields[s][c]
                north, south = vert[c][s]
                east, west = pltpu.roll(q, cols - 1, 1), pltpu.roll(q, 1, 1)
                out.append(
                    (north * cn + south * cs)
                    + (east * ce + west * cw)
                    - (4.0 * VISCOSITY) * q
                )
        return out

    def slopes(first, count, strips):
        def body(j, _):
            m = 2 * j
            one, two = node_slopes(m, strips), node_slopes(m + 1, strips)
            for b in range(2 * strips):
                both = jnp.concatenate([one[b], two[b]], axis=0)
                hi, lo = split2(both)
                at = pl.multiple_of(j * (2 * rows), 2 * rows)
                lanes = pl.ds(b * cols, cols)
                Sb[pl.ds(at, 2 * rows), lanes] = hi
                Sb[pl.ds(depth + at, 2 * rows), lanes] = lo
                Sb[pl.ds(2 * depth + at, 2 * rows), lanes] = hi
            return 0

        lax.fori_loop(first // 2, (first + count) // 2, body, 0, unroll=True)

    def integrate(strips):
        for b in range(2 * strips):
            s, c = divmod(b, 2)
            total = jnp.dot(
                T[...], Sb[:, b * cols : (b + 1) * cols], preferred_element_type=jnp.float32
            )
            X[s, :, c] = X[s, 0, c][None] + total.reshape(nodes, rows, cols)

    def restrict_lanes(stack):
        hi, lo = split2(stack)
        return jnp.dot(
            jnp.concatenate([hi, lo], axis=1), Rm[...], preferred_element_type=jnp.float32
        )

    for c in range(CHUNKS):
        loads[c].wait()
        swaps[c].wait_recv()
        slopes(c * per, per, 2)

    consts[0].wait()
    consts[1].wait()
    starts = restrict_lanes(
        jnp.concatenate([X[0, 0, 0], X[0, 0, 1], X[1, 0, 0], X[1, 0, 1]], axis=0)
    )
    sums = [row_sums(starts[8 * b : 8 * b + 8]) for b in range(4)]

    def ends_of(y):
        return [y[3:4], y[7:8]]

    su = jnp.concatenate((ends_of(sums[0]) + ends_of(sums[2])) * 2, axis=0)
    sv = jnp.concatenate((ends_of(sums[1]) + ends_of(sums[3])) * 2, axis=0)
    packed = jnp.where(left, su, sv)
    csend[...] = packed[0:4]

    def coarse_copy(t):
        return pltpu.make_async_remote_copy(
            src_ref=csend, dst_ref=coarse0, send_sem=cs_sem.at[t], recv_sem=cr_sem,
            device_id={"seg": t}, device_id_type=MESH,
        )

    gu, gv = coarse_prop(su, sv)
    gpack = jnp.where(left, gu, gv)

    consts[2].wait()
    integrate(2)
    slopes(0, nodes, 2)
    integrate(2)
    slopes(0, nodes, 1)

    @pl.when(seg < nseg - 1)
    def _():
        @pl.when(space == 0)
        def _():
            pl.semaphore_wait(barrier, 2 * (nseg - 1 - seg))
            pl.semaphore_signal(
                ready, inc=1, device_id={"space": 1}, device_id_type=MESH
            )

        @pl.when(space == 1)
        def _():
            pl.semaphore_wait(ready, 1)

    @pl.when(seg == 0)
    def _():
        for t in range(nseg - 1, 0, -1):
            coarse_copy(t).start()

    tail = jnp.dot(
        T[depth - 2 * rows :, :], Sb[:, : 2 * cols], preferred_element_type=jnp.float32
    )[rows:]
    eu = X[0, 0, 0] + tail[:, :cols]
    ev = X[0, 0, 1] + tail[:, cols:]
    ends[0] = eu
    ends[1] = ev
    finish = restrict_lanes(jnp.concatenate([eu, ev], axis=0))
    fpack = row_sums(jnp.where(left, finish[:8], finish[8:]))
    jsend[0:1] = fpack[3:4] - gpack[0:1]
    jsend[1:2] = fpack[7:8] - gpack[1:2]

    def jump_copy(t, s, way):
        return pltpu.make_async_remote_copy(
            src_ref=jsend, dst_ref=jumps.at[seg, way],
            send_sem=js_sem.at[t, way], recv_sem=jr_sem.at[seg, way],
            device_id={"seg": t, "space": s}, device_id_type=MESH,
        )

    def send_jump(i, _):
        t = nseg - 1 - i
        jump_copy(t, space, 0).start()
        jump_copy(t, other, 1).start()
        return 0

    lax.fori_loop(0, nseg - 1 - seg, send_jump, 0)

    end_copy = pltpu.make_async_remote_copy(
        src_ref=ends, dst_ref=prev, send_sem=ps_sem, recv_sem=pr_sem,
        device_id={"seg": lax.rem(seg + 1, nseg)}, device_id_type=MESH,
    )

    @pl.when(seg < nseg - 1)
    def _():
        end_copy.start()

    integrate(1)
    store = pltpu.make_async_copy(X.at[0], swept_hbm, osem)
    store.start()
    consts[3].wait()

    def expand(x):
        y = pltpu.roll(x, half, 1)
        return jnp.where(left, x, y), jnp.where(left, y, x)

    @pl.when(seg == 0)
    def _():
        shift_ref[...] = jnp.zeros_like(shift_ref)

    @pl.when(seg > 0)
    def _():
        coarse_copy(0).wait_recv()
        c = coarse0[...]
        u, v = expand(jnp.concatenate([c, c], axis=0))

        def advance(i, carry):
            u, v = coarse_prop(*carry)
            for way in range(2):
                pltpu.make_async_copy(jsend, jumps.at[i, way], jr_sem.at[i, way]).wait()
            own, oth = jumps[i, 0], jumps[i, 1]
            du, dv = expand(jnp.concatenate([own, oth, own, oth], axis=0))
            return u + du, v + dv

        u, v = lax.fori_loop(0, seg, advance, (u, v))
        end_copy.wait_recv()
        pu, pv = prev[0], prev[1]
        back = restrict_lanes(jnp.concatenate([pu, pv], axis=0))
        lower = lax.broadcasted_iota(jnp.int32, (8, 2 * half), 0) < 4
        spread = []
        for q, r in ((u, row_sums(back[:8])), (v, row_sums(back[8:]))):
            d0 = jnp.broadcast_to(q[0:1] - r[3:4], (8, 2 * half))
            d1 = jnp.broadcast_to(q[1:2] - r[7:8], (8, 2 * half))
            hi, lo = split2(jnp.where(lower, d0, d1))
            spread.append(
                jnp.where(left, hi.astype(jnp.float32), lo.astype(jnp.float32))
            )
        wide = jnp.dot(
            jnp.concatenate(spread, axis=0).astype(jnp.bfloat16), Pm[...],
            preferred_element_type=jnp.float32,
        )
        shift_ref[0] = (pu + wide[:8]) - X[0, 0, 0]
        shift_ref[1] = (pv + wide[8:]) - X[0, 0, 1]

    for copy in swaps:
        copy.wait_send()

    @pl.when(seg == 0)
    def _():
        for t in range(nseg - 1, 0, -1):
            coarse_copy(t).wait_send()

    def sent(i, _):
        t = nseg - 1 - i
        jump_copy(t, space, 0).wait_send()
        jump_copy(t, other, 1).wait_send()
        return 0

    lax.fori_loop(0, nseg - 1 - seg, sent, 0)

    @pl.when(seg < nseg - 1)
    def _():
        end_copy.wait_send()

    store.wait()


def per_device(nseg, trajectory):
    _, nodes, comps, rows, cols = trajectory.shape
    big, down, up = tables(nodes, rows, cols)
    depth = nodes * rows
    half = cols // COARSEN
    table = np.zeros((depth, 3 * depth + 4 * half + cols), big.dtype)
    table[:, : 3 * depth] = big
    table[:, 3 * depth : 3 * depth + 2 * half] = down[:cols]
    table[:, 3 * depth + 2 * half : 3 * depth + 4 * half] = down[cols:]
    table[: 2 * half, 3 * depth + 4 * half :] = up
    crows = rows // COARSEN
    bf16, f32 = jnp.bfloat16, jnp.float32
    DMA = pltpu.SemaphoreType.DMA
    anywhere = pl.BlockSpec(memory_space=pl.ANY)
    swept, shift = pl.pallas_call(
        functools.partial(kernel, nseg),
        out_shape=(
            jax.ShapeDtypeStruct((nodes, comps, rows, cols), f32),
            jax.ShapeDtypeStruct((comps, rows, cols), f32),
        ),
        in_specs=[anywhere] * 2,
        out_specs=(anywhere, pl.BlockSpec(memory_space=pltpu.VMEM)),
        scratch_shapes=[
            pltpu.VMEM((2, nodes, comps, rows, cols), f32),
            pltpu.VMEM((3 * depth, 2 * comps * cols), bf16),
            pltpu.VMEM(big.shape, bf16),
            pltpu.VMEM(down.shape, bf16),
            pltpu.VMEM(up.shape, bf16),
            pltpu.VMEM((2 * crows, 2 * half), f32),
            pltpu.VMEM((nseg, 2, crows, 2 * half), f32),
            pltpu.VMEM((comps, rows, cols), f32),
            pltpu.VMEM((crows, 2 * half), f32),
            pltpu.VMEM((2 * crows, 2 * half), f32),
            pltpu.VMEM((comps, rows, cols), f32),
            DMA((CHUNKS,)), DMA((4,)), DMA((CHUNKS,)), DMA((CHUNKS,)),
            DMA((nseg, 2)), DMA((nseg, 2)), DMA((nseg,)), DMA, DMA, DMA, DMA,
            pltpu.SemaphoreType.REGULAR, pltpu.SemaphoreType.REGULAR,
        ],
        compiler_params=pltpu.CompilerParams(
            collective_id=0, has_side_effects=True, vmem_limit_bytes=54400 * 1024
        ),
    )(trajectory, jnp.asarray(table))
    return (swept + shift[None])[None]


def solution(mesh):
    spec = P(("groups", "seg"), None, None, "space", None)
    return jax.shard_map(
        functools.partial(per_device, mesh.shape["seg"]),
        mesh=mesh,
        in_specs=(spec,),
        out_specs=spec,
        check_vma=False,
    )
```

```python
import functools

import jax
import jax.numpy as jnp
import ml_dtypes
import numpy as np
from jax import lax
from jax.experimental import pallas as pl
from jax.experimental.pallas import tpu as pltpu
from jax.sharding import PartitionSpec as P

SWEEPS = 3
CSTEPS = 4
COARSEN = 4
SEGMENT_TIME = 0.5
VISCOSITY = 0.05
MESH = pl.DeviceIdType.MESH
CHUNKS = 4


def integration_table(count, length):
    last = count - 1
    orders = np.arange(count)
    angles = np.pi * (last - orders) / last
    points = np.cos(angles)
    cheb = np.cos(np.outer(angles, orders))
    weights = np.where((orders == 0) | (orders == last), 0.5, 1.0)
    inverse = 2.0 / last * weights[:, None] * cheb.T * weights[None, :]
    upper = orders + 1.0
    lower = np.maximum(orders - 1.0, 1.0)
    general = np.cos(np.outer(angles, upper)) / (2.0 * upper) - np.cos(
        np.outer(angles, orders - 1.0)
    ) / (2.0 * lower)
    general = general - (
        (-1.0) ** (orders + 1) / (2.0 * upper) - (-1.0) ** np.abs(orders - 1) / (2.0 * lower)
    )
    integral = np.where(
        orders[None, :] == 0,
        points[:, None] + 1.0,
        np.where(orders[None, :] == 1, (points[:, None] ** 2 - 1.0) / 2.0, general),
    )
    return (integral @ inverse * (length / 2.0)).astype(np.float32)


def split2(x):
    hi = x.astype(jnp.bfloat16)
    lo = (x - hi.astype(jnp.float32)).astype(jnp.bfloat16)
    return hi, lo


def tables(nodes, rows, cols):
    table = integration_table(nodes, SEGMENT_TIME)
    hi = table.astype(ml_dtypes.bfloat16)
    lo = (table - hi.astype(np.float32)).astype(ml_dtypes.bfloat16)
    eye = np.eye(rows, dtype=np.float32)
    big_hi = np.kron(hi.astype(np.float32), eye)
    big_lo = np.kron(lo.astype(np.float32), eye)
    big = np.concatenate([big_hi, big_hi, big_lo], axis=1).astype(ml_dtypes.bfloat16)
    coarse = cols // COARSEN
    fine_of = np.arange(cols)[:, None] // COARSEN
    copies = np.arange(2 * coarse)[None, :] % coarse
    down = (fine_of == copies).astype(np.float32) / (COARSEN * COARSEN)
    down = np.concatenate([down, down], axis=0).astype(ml_dtypes.bfloat16)
    up = (fine_of == copies).astype(np.float32).T.astype(ml_dtypes.bfloat16)
    return big, down, up


def coarse_prop(u, v):
    step_len = SEGMENT_TIME / CSTEPS
    spacing = float(COARSEN)
    a = step_len * VISCOSITY / (spacing * spacing)
    b = step_len / (2.0 * spacing)
    lanes = u.shape[1]
    for _ in range(CSTEPS):
        bu, bv = b * u, b * v
        cn, cs, ce, cw = a - bu, a + bu, a - bv, a + bv
        both = []
        for q in (u, v):
            north, south = pltpu.roll(q, 7, 0), pltpu.roll(q, 1, 0)
            east, west = pltpu.roll(q, lanes - 1, 1), pltpu.roll(q, 1, 1)
            both.append(
                ((1.0 - 4.0 * a) * q + (north * cn + south * cs)) + (east * ce + west * cw)
            )
        u, v = both
    return u, v


def row_sums(y):
    y = y + pltpu.roll(y, 1, 0)
    return y + pltpu.roll(y, 2, 0)


def kernel(
    nseg, x_hbm, t_hbm, swept_hbm, shift_ref,
    X, Sb, T, Rm, Pm, coarse0, jumps, prev, jsend, csend, ends,
    lsem, csem, xs_sem, xr_sem, js_sem, jr_sem, cs_sem, cr_sem, ps_sem, pr_sem, osem,
    hello, ready,
):
    seg = lax.axis_index("seg")
    space = lax.axis_index("space")
    other = 1 - space
    nodes, cols = X.shape[1], X.shape[4]
    rows = X.shape[3]
    per = nodes // CHUNKS
    depth = nodes * rows
    half = Rm.shape[1] // 2

    loads = []
    for c in range(CHUNKS):
        part = pl.ds(c * per, per)
        loads.append(pltpu.make_async_copy(x_hbm.at[0, part], X.at[0, part], lsem.at[c]))
        loads[-1].start()
    wide, narrow = T.shape[1], Rm.shape[1]
    below = pl.ds(0, Pm.shape[0])
    consts = [
        pltpu.make_async_copy(
            t_hbm.at[:, pl.ds(wide, narrow)], Rm.at[pl.ds(0, cols)], csem.at[0]
        ),
        pltpu.make_async_copy(
            t_hbm.at[:, pl.ds(wide + narrow, narrow)], Rm.at[pl.ds(cols, cols)], csem.at[1]
        ),
        pltpu.make_async_copy(t_hbm.at[:, pl.ds(0, wide)], T, csem.at[2]),
        pltpu.make_async_copy(
            t_hbm.at[below, pl.ds(wide + 2 * narrow, cols)], Pm, csem.at[3]
        ),
    ]
    for copy in consts:
        copy.start()

    barrier = pltpu.get_barrier_semaphore()

    @pl.when(space == 0)
    def _():
        pl.semaphore_signal(
            barrier, inc=1, device_id={"space": 1}, device_id_type=MESH
        )

    def greet(t, _):
        pl.semaphore_signal(
            barrier, inc=1, device_id={"seg": t, "space": 0}, device_id_type=MESH
        )
        return 0

    lax.fori_loop(0, seg, greet, 0)

    @pl.when(space == 1)
    def _():
        pl.semaphore_wait(barrier, 1)
        pl.semaphore_signal(
            hello, inc=1, device_id={"space": 0}, device_id_type=MESH
        )

    @pl.when(space == 0)
    def _():
        pl.semaphore_wait(hello, 1)

    swaps = []
    for c in range(CHUNKS):
        part = pl.ds(c * per, per)
        swaps.append(
            pltpu.make_async_remote_copy(
                src_ref=x_hbm.at[0, part], dst_ref=X.at[1, part],
                send_sem=xs_sem.at[c], recv_sem=xr_sem.at[c],
                device_id={"space": other}, device_id_type=MESH,
            )
        )
        swaps[-1].start()

    row_id = lax.broadcasted_iota(jnp.int32, (rows, cols), 0)
    top, bottom = row_id == rows - 1, row_id == 0
    lane_id = lax.broadcasted_iota(jnp.int32, (8, 2 * half), 1)
    left = lane_id < half

    def slope_pair(q_own, q_oth):
        up_own, up_oth = pltpu.roll(q_own, rows - 1, 0), pltpu.roll(q_oth, rows - 1, 0)
        dn_own, dn_oth = pltpu.roll(q_own, 1, 0), pltpu.roll(q_oth, 1, 0)
        return (
            (jnp.where(top, up_oth, up_own), jnp.where(bottom, dn_oth, dn_own)),
            (jnp.where(top, up_own, up_oth), jnp.where(bottom, dn_own, dn_oth)),
        )

    def node_slopes(m, strips):
        fields = [[X[s, m, c] for c in range(2)] for s in range(2)]
        vert = [slope_pair(fields[0][c], fields[1][c]) for c in range(2)]
        out = []
        for s in range(strips):
            hu, hv = 0.5 * fields[s][0], 0.5 * fields[s][1]
            cn, cs, ce, cw = VISCOSITY - hu, VISCOSITY + hu, VISCOSITY - hv, VISCOSITY + hv
            for c in range(2):
                q = fields[s][c]
                north, south = vert[c][s]
                east, west = pltpu.roll(q, cols - 1, 1), pltpu.roll(q, 1, 1)
                out.append(
                    (north * cn + south * cs)
                    + (east * ce + west * cw)
                    - (4.0 * VISCOSITY) * q
                )
        return out

    def slopes(first, count, strips):
        def body(j, _):
            m = 2 * j
            one, two = node_slopes(m, strips), node_slopes(m + 1, strips)
            for b in range(2 * strips):
                both = jnp.concatenate([one[b], two[b]], axis=0)
                hi, lo = split2(both)
                at = pl.multiple_of(j * (2 * rows), 2 * rows)
                lanes = pl.ds(b * cols, cols)
                Sb[pl.ds(at, 2 * rows), lanes] = hi
                Sb[pl.ds(depth + at, 2 * rows), lanes] = lo
            return 0

        lax.fori_loop(first // 2, (first + count) // 2, body, 0, unroll=True)

    def integrate(strips):
        for b in range(2 * strips):
            s, c = divmod(b, 2)
            lanes = slice(b * cols, (b + 1) * cols)
            total = jnp.dot(
                T[:, : 2 * depth], Sb[:, lanes], preferred_element_type=jnp.float32
            ) + jnp.dot(
                T[:, 2 * depth :], Sb[:depth, lanes], preferred_element_type=jnp.float32
            )
            X[s, :, c] = X[s, 0, c][None] + total.reshape(nodes, rows, cols)

    def restrict_lanes(stack):
        hi, lo = split2(stack)
        return jnp.dot(
            jnp.concatenate([hi, lo], axis=1), Rm[...], preferred_element_type=jnp.float32
        )

    for c in range(CHUNKS):
        loads[c].wait()
        swaps[c].wait_recv()
        slopes(c * per, per, 2)

    consts[0].wait()
    consts[1].wait()
    starts = restrict_lanes(
        jnp.concatenate([X[0, 0, 0], X[0, 0, 1], X[1, 0, 0], X[1, 0, 1]], axis=0)
    )
    sums = [row_sums(starts[8 * b : 8 * b + 8]) for b in range(4)]

    def ends_of(y):
        return [y[3:4], y[7:8]]

    su = jnp.concatenate((ends_of(sums[0]) + ends_of(sums[2])) * 2, axis=0)
    sv = jnp.concatenate((ends_of(sums[1]) + ends_of(sums[3])) * 2, axis=0)
    packed = jnp.where(left, su, sv)
    csend[...] = packed[0:4]

    def coarse_copy(t):
        return pltpu.make_async_remote_copy(
            src_ref=csend, dst_ref=coarse0, send_sem=cs_sem.at[t], recv_sem=cr_sem,
            device_id={"seg": t}, device_id_type=MESH,
        )

    gu, gv = coarse_prop(su, sv)
    gpack = jnp.where(left, gu, gv)

    consts[2].wait()
    integrate(2)
    slopes(0, nodes, 2)
    integrate(2)
    slopes(0, nodes, 1)

    @pl.when(seg < nseg - 1)
    def _():
        @pl.when(space == 0)
        def _():
            pl.semaphore_wait(barrier, 2 * (nseg - 1 - seg))
            pl.semaphore_signal(
                ready, inc=1, device_id={"space": 1}, device_id_type=MESH
            )

        @pl.when(space == 1)
        def _():
            pl.semaphore_wait(ready, 1)

    @pl.when(seg == 0)
    def _():
        for t in range(nseg - 1, 0, -1):
            coarse_copy(t).start()

    tail = (
        jnp.dot(
            T[depth - 2 * rows :, : 2 * depth], Sb[:, : 2 * cols],
            preferred_element_type=jnp.float32,
        )
        + jnp.dot(
            T[depth - 2 * rows :, 2 * depth :], Sb[:depth, : 2 * cols],
            preferred_element_type=jnp.float32,
        )
    )[rows:]
    eu = X[0, 0, 0] + tail[:, :cols]
    ev = X[0, 0, 1] + tail[:, cols:]
    ends[0] = eu
    ends[1] = ev
    finish = restrict_lanes(jnp.concatenate([eu, ev], axis=0))
    fpack = row_sums(jnp.where(left, finish[:8], finish[8:]))
    jsend[0:1] = fpack[3:4] - gpack[0:1]
    jsend[1:2] = fpack[7:8] - gpack[1:2]

    def jump_copy(t, s, way):
        return pltpu.make_async_remote_copy(
            src_ref=jsend, dst_ref=jumps.at[seg, way],
            send_sem=js_sem.at[t, way], recv_sem=jr_sem.at[seg, way],
            device_id={"seg": t, "space": s}, device_id_type=MESH,
        )

    def send_jump(i, _):
        t = nseg - 1 - i
        jump_copy(t, space, 0).start()
        jump_copy(t, other, 1).start()
        return 0

    lax.fori_loop(0, nseg - 1 - seg, send_jump, 0)

    end_copy = pltpu.make_async_remote_copy(
        src_ref=ends, dst_ref=prev, send_sem=ps_sem, recv_sem=pr_sem,
        device_id={"seg": lax.rem(seg + 1, nseg)}, device_id_type=MESH,
    )

    @pl.when(seg < nseg - 1)
    def _():
        end_copy.start()

    integrate(1)
    store = pltpu.make_async_copy(X.at[0], swept_hbm, osem)
    store.start()
    consts[3].wait()

    def expand(x):
        y = pltpu.roll(x, half, 1)
        return jnp.where(left, x, y), jnp.where(left, y, x)

    @pl.when(seg == 0)
    def _():
        shift_ref[...] = jnp.zeros_like(shift_ref)

    @pl.when(seg > 0)
    def _():
        coarse_copy(0).wait_recv()
        c = coarse0[...]
        u, v = expand(jnp.concatenate([c, c], axis=0))

        def advance(i, carry):
            u, v = coarse_prop(*carry)
            for way in range(2):
                pltpu.make_async_copy(jsend, jumps.at[i, way], jr_sem.at[i, way]).wait()
            own, oth = jumps[i, 0], jumps[i, 1]
            du, dv = expand(jnp.concatenate([own, oth, own, oth], axis=0))
            return u + du, v + dv

        u, v = lax.fori_loop(0, seg, advance, (u, v))
        end_copy.wait_recv()
        pu, pv = prev[0], prev[1]
        back = restrict_lanes(jnp.concatenate([pu, pv], axis=0))
        lower = lax.broadcasted_iota(jnp.int32, (8, 2 * half), 0) < 4
        spread = []
        for q, r in ((u, row_sums(back[:8])), (v, row_sums(back[8:]))):
            d0 = jnp.broadcast_to(q[0:1] - r[3:4], (8, 2 * half))
            d1 = jnp.broadcast_to(q[1:2] - r[7:8], (8, 2 * half))
            hi, lo = split2(jnp.where(lower, d0, d1))
            spread.append(
                jnp.where(left, hi.astype(jnp.float32), lo.astype(jnp.float32))
            )
        wide = jnp.dot(
            jnp.concatenate(spread, axis=0).astype(jnp.bfloat16), Pm[...],
            preferred_element_type=jnp.float32,
        )
        shift_ref[0] = (pu + wide[:8]) - X[0, 0, 0]
        shift_ref[1] = (pv + wide[8:]) - X[0, 0, 1]

    for copy in swaps:
        copy.wait_send()

    @pl.when(seg == 0)
    def _():
        for t in range(nseg - 1, 0, -1):
            coarse_copy(t).wait_send()

    def sent(i, _):
        t = nseg - 1 - i
        jump_copy(t, space, 0).wait_send()
        jump_copy(t, other, 1).wait_send()
        return 0

    lax.fori_loop(0, nseg - 1 - seg, sent, 0)

    @pl.when(seg < nseg - 1)
    def _():
        end_copy.wait_send()

    store.wait()


def per_device(nseg, trajectory):
    _, nodes, comps, rows, cols = trajectory.shape
    big, down, up = tables(nodes, rows, cols)
    depth = nodes * rows
    half = cols // COARSEN
    table = np.zeros((depth, 3 * depth + 4 * half + cols), big.dtype)
    table[:, : 3 * depth] = big
    table[:, 3 * depth : 3 * depth + 2 * half] = down[:cols]
    table[:, 3 * depth + 2 * half : 3 * depth + 4 * half] = down[cols:]
    table[: 2 * half, 3 * depth + 4 * half :] = up
    crows = rows // COARSEN
    bf16, f32 = jnp.bfloat16, jnp.float32
    DMA = pltpu.SemaphoreType.DMA
    anywhere = pl.BlockSpec(memory_space=pl.ANY)
    swept, shift = pl.pallas_call(
        functools.partial(kernel, nseg),
        out_shape=(
            jax.ShapeDtypeStruct((nodes, comps, rows, cols), f32),
            jax.ShapeDtypeStruct((comps, rows, cols), f32),
        ),
        in_specs=[anywhere] * 2,
        out_specs=(anywhere, pl.BlockSpec(memory_space=pltpu.VMEM)),
        scratch_shapes=[
            pltpu.VMEM((2, nodes, comps, rows, cols), f32),
            pltpu.VMEM((2 * depth, 2 * comps * cols), bf16),
            pltpu.VMEM(big.shape, bf16),
            pltpu.VMEM(down.shape, bf16),
            pltpu.VMEM(up.shape, bf16),
            pltpu.VMEM((2 * crows, 2 * half), f32),
            pltpu.VMEM((nseg, 2, crows, 2 * half), f32),
            pltpu.VMEM((comps, rows, cols), f32),
            pltpu.VMEM((crows, 2 * half), f32),
            pltpu.VMEM((2 * crows, 2 * half), f32),
            pltpu.VMEM((comps, rows, cols), f32),
            DMA((CHUNKS,)), DMA((4,)), DMA((CHUNKS,)), DMA((CHUNKS,)),
            DMA((nseg, 2)), DMA((nseg, 2)), DMA((nseg,)), DMA, DMA, DMA, DMA,
            pltpu.SemaphoreType.REGULAR, pltpu.SemaphoreType.REGULAR,
        ],
        compiler_params=pltpu.CompilerParams(
            collective_id=0, has_side_effects=True, vmem_limit_bytes=54400 * 1024
        ),
    )(trajectory, jnp.asarray(table))
    return (swept + shift[None])[None]


def solution(mesh):
    spec = P(("groups", "seg"), None, None, "space", None)
    return jax.shard_map(
        functools.partial(per_device, mesh.shape["seg"]),
        mesh=mesh,
        in_specs=(spec,),
        out_specs=spec,
        check_vma=False,
    )
```

```python
import functools

import jax
import jax.numpy as jnp
import ml_dtypes
import numpy as np
from jax import lax
from jax.experimental import pallas as pl
from jax.experimental.pallas import tpu as pltpu
from jax.sharding import PartitionSpec as P

SWEEPS = 3
CSTEPS = 4
COARSEN = 4
SEGMENT_TIME = 0.5
VISCOSITY = 0.05
MESH = pl.DeviceIdType.MESH
CHUNKS = 4


def integration_table(count, length):
    last = count - 1
    orders = np.arange(count)
    angles = np.pi * (last - orders) / last
    points = np.cos(angles)
    cheb = np.cos(np.outer(angles, orders))
    weights = np.where((orders == 0) | (orders == last), 0.5, 1.0)
    inverse = 2.0 / last * weights[:, None] * cheb.T * weights[None, :]
    upper = orders + 1.0
    lower = np.maximum(orders - 1.0, 1.0)
    general = np.cos(np.outer(angles, upper)) / (2.0 * upper) - np.cos(
        np.outer(angles, orders - 1.0)
    ) / (2.0 * lower)
    general = general - (
        (-1.0) ** (orders + 1) / (2.0 * upper) - (-1.0) ** np.abs(orders - 1) / (2.0 * lower)
    )
    integral = np.where(
        orders[None, :] == 0,
        points[:, None] + 1.0,
        np.where(orders[None, :] == 1, (points[:, None] ** 2 - 1.0) / 2.0, general),
    )
    return (integral @ inverse * (length / 2.0)).astype(np.float32)


def split2(x):
    hi = x.astype(jnp.bfloat16)
    lo = (x - hi.astype(jnp.float32)).astype(jnp.bfloat16)
    return hi, lo


def tables(nodes, rows, cols):
    table = integration_table(nodes, SEGMENT_TIME)
    hi = table.astype(ml_dtypes.bfloat16)
    lo = (table - hi.astype(np.float32)).astype(ml_dtypes.bfloat16)
    eye = np.eye(rows, dtype=np.float32)
    big_hi = np.kron(hi.astype(np.float32), eye)
    big_lo = np.kron(lo.astype(np.float32), eye)
    big = np.concatenate([big_hi, big_hi, big_lo], axis=1).astype(ml_dtypes.bfloat16)
    coarse = cols // COARSEN
    fine_of = np.arange(cols)[:, None] // COARSEN
    copies = np.arange(2 * coarse)[None, :] % coarse
    down = (fine_of == copies).astype(np.float32) / (COARSEN * COARSEN)
    down = np.concatenate([down, down], axis=0).astype(ml_dtypes.bfloat16)
    up = (fine_of == copies).astype(np.float32).T.astype(ml_dtypes.bfloat16)
    return big, down, up


def coarse_prop(u, v):
    step_len = SEGMENT_TIME / CSTEPS
    spacing = float(COARSEN)
    a = step_len * VISCOSITY / (spacing * spacing)
    b = step_len / (2.0 * spacing)
    lanes = u.shape[1]
    for _ in range(CSTEPS):
        bu, bv = b * u, b * v
        cn, cs, ce, cw = a - bu, a + bu, a - bv, a + bv
        both = []
        for q in (u, v):
            north, south = pltpu.roll(q, 7, 0), pltpu.roll(q, 1, 0)
            east, west = pltpu.roll(q, lanes - 1, 1), pltpu.roll(q, 1, 1)
            both.append(
                ((1.0 - 4.0 * a) * q + (north * cn + south * cs)) + (east * ce + west * cw)
            )
        u, v = both
    return u, v


def row_sums(y):
    y = y + pltpu.roll(y, 1, 0)
    return y + pltpu.roll(y, 2, 0)


def kernel(
    nseg, x_hbm, t_hbm, swept_hbm, shift_ref,
    X, Sb, T, Rm, Pm, coarse0, jumps, prev, jsend, csend, ends,
    lsem, csem, xs_sem, xr_sem, js_sem, jr_sem, cs_sem, cr_sem, ps_sem, pr_sem, osem,
    hello, ready,
):
    seg = lax.axis_index("seg")
    space = lax.axis_index("space")
    other = 1 - space
    nodes, cols = X.shape[1], X.shape[4]
    rows = X.shape[3]
    per = nodes // CHUNKS
    depth = nodes * rows
    half = Rm.shape[1] // 2

    loads = []
    for c in range(CHUNKS):
        part = pl.ds(c * per, per)
        loads.append(pltpu.make_async_copy(x_hbm.at[0, part], X.at[0, part], lsem.at[c]))
        loads[-1].start()
    wide, narrow = T.shape[1], Rm.shape[1]
    below = pl.ds(0, Pm.shape[0])
    consts = [
        pltpu.make_async_copy(
            t_hbm.at[:, pl.ds(wide, narrow)], Rm.at[pl.ds(0, cols)], csem.at[0]
        ),
        pltpu.make_async_copy(
            t_hbm.at[:, pl.ds(wide + narrow, narrow)], Rm.at[pl.ds(cols, cols)], csem.at[1]
        ),
        pltpu.make_async_copy(t_hbm.at[:, pl.ds(0, wide)], T, csem.at[2]),
        pltpu.make_async_copy(
            t_hbm.at[below, pl.ds(wide + 2 * narrow, cols)], Pm, csem.at[3]
        ),
    ]
    for copy in consts:
        copy.start()

    barrier = pltpu.get_barrier_semaphore()

    @pl.when(space == 0)
    def _():
        pl.semaphore_signal(
            barrier, inc=1, device_id={"space": 1}, device_id_type=MESH
        )

    def greet(t, _):
        pl.semaphore_signal(
            barrier, inc=1, device_id={"seg": t, "space": 0}, device_id_type=MESH
        )
        return 0

    lax.fori_loop(0, seg, greet, 0)

    @pl.when(space == 1)
    def _():
        pl.semaphore_wait(barrier, 1)
        pl.semaphore_signal(
            hello, inc=1, device_id={"space": 0}, device_id_type=MESH
        )

    @pl.when(space == 0)
    def _():
        pl.semaphore_wait(hello, 1)

    swaps = []
    for c in range(CHUNKS):
        part = pl.ds(c * per, per)
        swaps.append(
            pltpu.make_async_remote_copy(
                src_ref=x_hbm.at[0, part], dst_ref=X.at[1, part],
                send_sem=xs_sem.at[c], recv_sem=xr_sem.at[c],
                device_id={"space": other}, device_id_type=MESH,
            )
        )
        swaps[-1].start()

    row_id = lax.broadcasted_iota(jnp.int32, (rows, cols), 0)
    top, bottom = row_id == rows - 1, row_id == 0
    lane_id = lax.broadcasted_iota(jnp.int32, (8, 2 * half), 1)
    left = lane_id < half

    def slope_pair(q_own, q_oth):
        up_own, up_oth = pltpu.roll(q_own, rows - 1, 0), pltpu.roll(q_oth, rows - 1, 0)
        dn_own, dn_oth = pltpu.roll(q_own, 1, 0), pltpu.roll(q_oth, 1, 0)
        return (
            (jnp.where(top, up_oth, up_own), jnp.where(bottom, dn_oth, dn_own)),
            (jnp.where(top, up_own, up_oth), jnp.where(bottom, dn_own, dn_oth)),
        )

    def node_slopes(m, strips):
        fields = [[X[s, m, c] for c in range(2)] for s in range(2)]
        vert = [slope_pair(fields[0][c], fields[1][c]) for c in range(2)]
        out = []
        for s in range(strips):
            hu, hv = 0.5 * fields[s][0], 0.5 * fields[s][1]
            cn, cs, ce, cw = VISCOSITY - hu, VISCOSITY + hu, VISCOSITY - hv, VISCOSITY + hv
            for c in range(2):
                q = fields[s][c]
                north, south = vert[c][s]
                east, west = pltpu.roll(q, cols - 1, 1), pltpu.roll(q, 1, 1)
                out.append(
                    (north * cn + south * cs)
                    + (east * ce + west * cw)
                    - (4.0 * VISCOSITY) * q
                )
        return out

    def slopes(first, count, strips):
        def body(j, _):
            m = 2 * j
            one, two = node_slopes(m, strips), node_slopes(m + 1, strips)
            for b in range(2 * strips):
                both = jnp.concatenate([one[b], two[b]], axis=0)
                hi, lo = split2(both)
                at = pl.multiple_of(j * (2 * rows), 2 * rows)
                lanes = pl.ds(b * cols, cols)
                Sb[pl.ds(at, 2 * rows), lanes] = hi
                Sb[pl.ds(depth + at, 2 * rows), lanes] = lo
            return 0

        lax.fori_loop(first // 2, (first + count) // 2, body, 0, unroll=True)

    def integrate(strips):
        for b in range(2 * strips):
            s, c = divmod(b, 2)
            lanes = slice(b * cols, (b + 1) * cols)
            total = jnp.dot(
                T[:, : 2 * depth], Sb[:, lanes], preferred_element_type=jnp.float32
            ) + jnp.dot(
                T[:, 2 * depth :], Sb[:depth, lanes], preferred_element_type=jnp.float32
            )
            X[s, :, c] = X[s, 0, c][None] + total.reshape(nodes, rows, cols)

    def restrict_lanes(stack):
        hi, lo = split2(stack)
        return jnp.dot(
            jnp.concatenate([hi, lo], axis=1), Rm[...], preferred_element_type=jnp.float32
        )

    for c in range(CHUNKS):
        loads[c].wait()
        swaps[c].wait_recv()
        slopes(c * per, per, 2)

    consts[0].wait()
    consts[1].wait()
    starts = restrict_lanes(
        jnp.concatenate([X[0, 0, 0], X[0, 0, 1], X[1, 0, 0], X[1, 0, 1]], axis=0)
    )
    sums = [row_sums(starts[8 * b : 8 * b + 8]) for b in range(4)]

    def ends_of(y):
        return [y[3:4], y[7:8]]

    su = jnp.concatenate((ends_of(sums[0]) + ends_of(sums[2])) * 2, axis=0)
    sv = jnp.concatenate((ends_of(sums[1]) + ends_of(sums[3])) * 2, axis=0)
    packed = jnp.where(left, su, sv)
    csend[...] = packed[0:4]

    def coarse_copy(t):
        return pltpu.make_async_remote_copy(
            src_ref=csend, dst_ref=coarse0, send_sem=cs_sem.at[t], recv_sem=cr_sem,
            device_id={"seg": t}, device_id_type=MESH,
        )

    gu, gv = coarse_prop(su, sv)
    gpack = jnp.where(left, gu, gv)

    consts[2].wait()
    integrate(2)
    slopes(0, nodes, 2)
    integrate(2)
    @pl.when(seg < nseg - 1)
    def _():
        @pl.when(space == 0)
        def _():
            pl.semaphore_wait(barrier, 2 * (nseg - 1 - seg))
            pl.semaphore_signal(
                ready, inc=1, device_id={"space": 1}, device_id_type=MESH
            )

        @pl.when(space == 1)
        def _():
            pl.semaphore_wait(ready, 1)

    @pl.when(seg == 0)
    def _():
        for t in range(nseg - 1, 0, -1):
            coarse_copy(t).start()

    slopes(0, nodes, 1)

    tail = (
        jnp.dot(
            T[depth - 2 * rows :, : 2 * depth], Sb[:, : 2 * cols],
            preferred_element_type=jnp.float32,
        )
        + jnp.dot(
            T[depth - 2 * rows :, 2 * depth :], Sb[:depth, : 2 * cols],
            preferred_element_type=jnp.float32,
        )
    )[rows:]
    eu = X[0, 0, 0] + tail[:, :cols]
    ev = X[0, 0, 1] + tail[:, cols:]
    ends[0] = eu
    ends[1] = ev
    finish = restrict_lanes(jnp.concatenate([eu, ev], axis=0))
    fpack = row_sums(jnp.where(left, finish[:8], finish[8:]))
    jsend[0:1] = fpack[3:4] - gpack[0:1]
    jsend[1:2] = fpack[7:8] - gpack[1:2]

    def jump_copy(t, s, way):
        return pltpu.make_async_remote_copy(
            src_ref=jsend, dst_ref=jumps.at[seg, way],
            send_sem=js_sem.at[t, way], recv_sem=jr_sem.at[seg, way],
            device_id={"seg": t, "space": s}, device_id_type=MESH,
        )

    def send_jump(i, _):
        t = nseg - 1 - i
        jump_copy(t, space, 0).start()
        jump_copy(t, other, 1).start()
        return 0

    lax.fori_loop(0, nseg - 1 - seg, send_jump, 0)

    end_copy = pltpu.make_async_remote_copy(
        src_ref=ends, dst_ref=prev, send_sem=ps_sem, recv_sem=pr_sem,
        device_id={"seg": lax.rem(seg + 1, nseg)}, device_id_type=MESH,
    )

    @pl.when(seg < nseg - 1)
    def _():
        end_copy.start()

    integrate(1)
    store = pltpu.make_async_copy(X.at[0], swept_hbm, osem)
    store.start()
    consts[3].wait()

    def expand(x):
        y = pltpu.roll(x, half, 1)
        return jnp.where(left, x, y), jnp.where(left, y, x)

    @pl.when(seg == 0)
    def _():
        shift_ref[...] = jnp.zeros_like(shift_ref)

    @pl.when(seg > 0)
    def _():
        coarse_copy(0).wait_recv()
        c = coarse0[...]
        u, v = expand(jnp.concatenate([c, c], axis=0))

        def advance(i, carry):
            u, v = coarse_prop(*carry)
            for way in range(2):
                pltpu.make_async_copy(jsend, jumps.at[i, way], jr_sem.at[i, way]).wait()
            own, oth = jumps[i, 0], jumps[i, 1]
            du, dv = expand(jnp.concatenate([own, oth, own, oth], axis=0))
            return u + du, v + dv

        u, v = lax.fori_loop(0, seg, advance, (u, v))
        end_copy.wait_recv()
        pu, pv = prev[0], prev[1]
        back = restrict_lanes(jnp.concatenate([pu, pv], axis=0))
        lower = lax.broadcasted_iota(jnp.int32, (8, 2 * half), 0) < 4
        spread = []
        for q, r in ((u, row_sums(back[:8])), (v, row_sums(back[8:]))):
            d0 = jnp.broadcast_to(q[0:1] - r[3:4], (8, 2 * half))
            d1 = jnp.broadcast_to(q[1:2] - r[7:8], (8, 2 * half))
            hi, lo = split2(jnp.where(lower, d0, d1))
            spread.append(
                jnp.where(left, hi.astype(jnp.float32), lo.astype(jnp.float32))
            )
        wide = jnp.dot(
            jnp.concatenate(spread, axis=0).astype(jnp.bfloat16), Pm[...],
            preferred_element_type=jnp.float32,
        )
        shift_ref[0] = (pu + wide[:8]) - X[0, 0, 0]
        shift_ref[1] = (pv + wide[8:]) - X[0, 0, 1]

    for copy in swaps:
        copy.wait_send()

    @pl.when(seg == 0)
    def _():
        for t in range(nseg - 1, 0, -1):
            coarse_copy(t).wait_send()

    def sent(i, _):
        t = nseg - 1 - i
        jump_copy(t, space, 0).wait_send()
        jump_copy(t, other, 1).wait_send()
        return 0

    lax.fori_loop(0, nseg - 1 - seg, sent, 0)

    @pl.when(seg < nseg - 1)
    def _():
        end_copy.wait_send()

    store.wait()


def per_device(nseg, trajectory):
    _, nodes, comps, rows, cols = trajectory.shape
    big, down, up = tables(nodes, rows, cols)
    depth = nodes * rows
    half = cols // COARSEN
    table = np.zeros((depth, 3 * depth + 4 * half + cols), big.dtype)
    table[:, : 3 * depth] = big
    table[:, 3 * depth : 3 * depth + 2 * half] = down[:cols]
    table[:, 3 * depth + 2 * half : 3 * depth + 4 * half] = down[cols:]
    table[: 2 * half, 3 * depth + 4 * half :] = up
    crows = rows // COARSEN
    bf16, f32 = jnp.bfloat16, jnp.float32
    DMA = pltpu.SemaphoreType.DMA
    anywhere = pl.BlockSpec(memory_space=pl.ANY)
    swept, shift = pl.pallas_call(
        functools.partial(kernel, nseg),
        out_shape=(
            jax.ShapeDtypeStruct((nodes, comps, rows, cols), f32),
            jax.ShapeDtypeStruct((comps, rows, cols), f32),
        ),
        in_specs=[anywhere] * 2,
        out_specs=(anywhere, pl.BlockSpec(memory_space=pltpu.VMEM)),
        scratch_shapes=[
            pltpu.VMEM((2, nodes, comps, rows, cols), f32),
            pltpu.VMEM((2 * depth, 2 * comps * cols), bf16),
            pltpu.VMEM(big.shape, bf16),
            pltpu.VMEM(down.shape, bf16),
            pltpu.VMEM(up.shape, bf16),
            pltpu.VMEM((2 * crows, 2 * half), f32),
            pltpu.VMEM((nseg, 2, crows, 2 * half), f32),
            pltpu.VMEM((comps, rows, cols), f32),
            pltpu.VMEM((crows, 2 * half), f32),
            pltpu.VMEM((2 * crows, 2 * half), f32),
            pltpu.VMEM((comps, rows, cols), f32),
            DMA((CHUNKS,)), DMA((4,)), DMA((CHUNKS,)), DMA((CHUNKS,)),
            DMA((nseg, 2)), DMA((nseg, 2)), DMA((nseg,)), DMA, DMA, DMA, DMA,
            pltpu.SemaphoreType.REGULAR, pltpu.SemaphoreType.REGULAR,
        ],
        compiler_params=pltpu.CompilerParams(
            collective_id=0, has_side_effects=True, vmem_limit_bytes=54400 * 1024
        ),
    )(trajectory, jnp.asarray(table))
    return (swept + shift[None])[None]


def solution(mesh):
    spec = P(("groups", "seg"), None, None, "space", None)
    return jax.shard_map(
        functools.partial(per_device, mesh.shape["seg"]),
        mesh=mesh,
        in_specs=(spec,),
        out_specs=spec,
        check_vma=False,
    )
```
